256 devices in a mesh: mesh: 64 (over z, y, core), samp: 4 (over x).
Axes of the slice: x: 4, y: 4, z: 8, core: 2. Of those that a mesh axis runs over, the one named last changes fastest.
Arguments:
- traces: bfloat16 [320, 128, 8192], P('mesh', None, 'samp'), may hold values from -6 to 6
- sketch: bfloat16 [8192, 256], P('samp'), may hold values from -0.0625 to 0.0625
- face_port: int32 [320], P('mesh'), may hold values from 0 to 63, as said below
- face_pos: int32 [320], P('mesh'), may hold values from 0 to 3
- tile_count: int32 [64], P('mesh'), may hold values from 0 to 5, as said below
- port_owner: int32 [64], replicated, may hold values from 0 to 63, as said below
Outputs:
- port_bases: float32 [128, 512, 256], P('mesh')
The draws below stay inside these ranges and needn't reach their ends.
Inputs may be any that keep to these rules, and one draw needn't show every extreme that they name: Ports are numbered like slabs. The used tiles of port p lie on 4 of the 5 slabs p, p + 1, ..., p + 4 (mod 64), one tile on each, positions 0 to 3 rising with the slab. Used slots of a slab come first, in order of rising port distance; unused slots hold 0 in face_port and face_pos. `tile_count`: some slab uses all its slots. `port_owner`: the owner of port p is slab p + 1 or p + 2 (mod 64). No device owns more than 2 ports, and some device owns exactly 2; some slab sends exactly 2 used tiles to one owner.
All inputs are finite; a program needn't handle non-finite values.
Results may differ from the reference program's by a relative error of at most 0.0038.
Values may be sent and summed in bfloat16 or wider, within the bound.
No kernel may reach another device: no remote copies, remote signals or barrier semaphores. Data moves between devices by JAX's collectives and lax.ppermute only.
A program may use at most 64 MiB of HBM per device.

```python
import jax
import jax.numpy as jnp
from jax import lax

FACE_CELLS = 128
RANK = 256
FACES = 4
PORT_MOST = 2
TILE_SLOTS = 5
PORTS = 64
SAMPLES = 8192
N_MESH = 64


def port_plan(key):
    plan_key = jax.random.fold_in(key, 11)
    key_skip, key_home, key_lean = jax.random.split(plan_key, 3)
    port_ids = jnp.arange(PORTS, dtype=jnp.int32)
    home = jax.random.randint(key_home, (), 0, PORTS).astype(jnp.int32)
    skipped = jax.random.randint(key_skip, (PORTS,), 0, TILE_SLOTS).astype(jnp.int32)
    offset_home = (home - port_ids) % PORTS
    near_home = offset_home < TILE_SLOTS
    skipped = jnp.where(near_home & (skipped == offset_home), (offset_home + 1) % TILE_SLOTS, skipped)
    leaning = jax.random.randint(key_lean, (PORTS,), 1, 3).astype(jnp.int32)
    leaning = jnp.where(port_ids == (home - 1) % PORTS, 1, leaning)
    leaning = jnp.where(port_ids == (home - 2) % PORTS, 2, leaning)
    return (skipped.astype(jnp.int32), leaning.astype(jnp.int32))


def port_layout(key):
    skipped, leaning = port_plan(key)
    offsets_row = jnp.arange(TILE_SLOTS, dtype=jnp.int32)
    keeping = (offsets_row[None, :] != skipped[:, None]).astype(jnp.int32)
    ordinal = jnp.cumsum(keeping, axis=1) - 1
    devices = jnp.arange(N_MESH, dtype=jnp.int32)[:, None]
    offsets = offsets_row[None, :]
    port_at = (devices - offsets) % PORTS
    present = keeping[port_at, offsets]
    ordinal_at = ordinal[port_at, offsets]
    slot_index = jnp.cumsum(present, axis=1) - 1
    onehot = ((slot_index[:, :, None] == offsets_row[None, None, :]) & (present[:, :, None] == 1)).astype(jnp.int32)
    port_list = jnp.sum(onehot * port_at[:, :, None], axis=1).reshape(-1)
    position_list = jnp.sum(onehot * ordinal_at[:, :, None], axis=1).reshape(-1)
    counts = jnp.sum(present, axis=1)
    return (port_list, position_list, counts)


def draw_face_port(key, part):
    layout = port_layout(key)
    return layout[0].astype(jnp.int32)


def draw_face_pos(key, part):
    layout = port_layout(key)
    return layout[1].astype(jnp.int32)


def draw_tile_count(key, part):
    layout = port_layout(key)
    return layout[2].astype(jnp.int32)


def draw_port_owner(key, part):
    skipped, leaning = port_plan(key)
    port_ids = jnp.arange(PORTS, dtype=jnp.int32)
    return ((port_ids + leaning) % N_MESH).astype(jnp.int32)


def levels(key, dims, cuts, smallest, largest):
    def one(dim, shards_of):
        draws = jax.random.uniform(jax.random.fold_in(jax.random.fold_in(key, 6), dim), (shards_of,), jnp.float32, smallest / len(cuts), largest / len(cuts))
        return jnp.repeat(jnp.exp(draws), dims[dim] // shards_of).reshape((-1,) + (1,) * (len(dims) - dim - 1))

    level = one(*cuts[0])
    for cut in cuts[1:]:
        level = level * one(*cut)
    return level


def noise(stream_key, extent, scale, reach, pieces=(), kind=jnp.bfloat16):
    result = scale * jax.random.normal(stream_key, extent, jnp.float32)
    if pieces:
        result = result * levels(stream_key, extent, pieces, -0.22, 0.18)
    return jnp.clip(result, -reach, reach).astype(kind)


def setup_inputs(seed: int = 0) -> dict:
    seeds = jax.random.split(jax.random.key(seed), 7)
    return {
        "traces": noise(seeds[0], (N_MESH * TILE_SLOTS, FACE_CELLS, SAMPLES), 1.0, 6.0, ((0, 64), (2, 4))),
        "sketch": noise(seeds[1], (SAMPLES, RANK), SAMPLES ** -0.5, 0.0625, ((0, 4),)),
        "face_port": draw_face_port(jax.random.fold_in(seeds[6], 71), 0),
        "face_pos": draw_face_pos(jax.random.fold_in(seeds[6], 71), 0),
        "tile_count": draw_tile_count(jax.random.fold_in(seeds[6], 71), 0),
        "port_owner": draw_port_owner(jax.random.fold_in(seeds[6], 71), 0),
    }


def orthonormal(port_block):
    gram_matrix = jnp.dot(port_block.T.astype(jnp.float32), port_block.astype(jnp.float32), preferred_element_type=jnp.float32)
    diagonal_shift = 0.1 * jnp.trace(gram_matrix) / RANK + 1e-06
    factor = jnp.linalg.cholesky(gram_matrix + diagonal_shift * jnp.eye(RANK, dtype=jnp.float32))
    return lax.linalg.triangular_solve(factor, port_block.astype(jnp.float32), left_side=False, lower=True, transpose_a=True)

def reference(traces, sketch, face_port, face_pos, tile_count, port_owner):
    slot_total = traces.shape[0]
    flattened = traces.reshape(slot_total * FACE_CELLS, SAMPLES)
    partial_sum = jnp.dot(flattened.astype(jnp.float32), sketch.astype(jnp.float32), preferred_element_type=jnp.float32)
    face_sketch = partial_sum.astype(jnp.bfloat16).reshape(slot_total, FACE_CELLS, RANK)
    slot_ids = jnp.arange(slot_total, dtype=jnp.int32)
    used = slot_ids % TILE_SLOTS < tile_count[slot_ids // TILE_SLOTS]
    targets = jnp.where(used, face_port * FACES + face_pos, PORTS * FACES).astype(jnp.int32)
    face_blocks = jnp.zeros((PORTS * FACES + 1, FACE_CELLS, RANK), jnp.bfloat16).at[targets].set(face_sketch)
    port_sketch = face_blocks[:PORTS * FACES].reshape(PORTS, FACES * FACE_CELLS, RANK)
    bases = lax.map(orthonormal, port_sketch)
    port_ids = jnp.arange(PORTS, dtype=jnp.int32)
    earlier = (port_owner[None, :] == port_owner[:, None]) & (port_ids[None, :] < port_ids[:, None])
    owner_rank = jnp.sum(earlier.astype(jnp.int32), axis=1)
    destination = (port_owner * PORT_MOST + owner_rank).astype(jnp.int32)
    result_bases = jnp.zeros((N_MESH * PORT_MOST, FACES * FACE_CELLS, RANK), jnp.float32)
    return result_bases.at[destination].set(bases)
```

```python
import jax
import jax.numpy as jnp
from jax import lax
from jax.experimental import pallas as pl
from jax.experimental.pallas import tpu as pltpu
from jax.sharding import PartitionSpec as P

FACES = 4
PORT_MOST = 2


def passed_along(block, axis, distance):
    devices = range(lax.axis_size(axis))
    route = [((i - distance) % len(devices), i) for i in devices]
    return lax.ppermute(block, axis, route)


B = 64
HI = lax.Precision.HIGHEST
f32 = jnp.float32

def mm(a, b, dims=((1,), (0,)), prec=HI):
    return lax.dot_general(a, b, (dims, ((), ())), precision=prec, preferred_element_type=f32)

def panel(t0):
    lane = lax.broadcasted_iota(jnp.int32, (B, 128), 1)
    row = lax.broadcasted_iota(jnp.int32, (B, 128), 0)
    t1 = ((lane % B) == row).astype(f32)
    half = jnp.where(lane < B, 0, B)
    r0 = [t0[8*i:8*i+8] for i in range(B//8)]
    r1 = [t1[8*i:8*i+8] for i in range(B//8)]
    h8 = half[:8]
    row8 = row[:8]
    done = []
    for g in range(B//8):
        n = B//8 - g
        C = [[jnp.take_along_axis(r0[g+i], h8 + (8*g+j), axis=1, mode="promise_in_bounds") for i in range(n)] for j in range(8)]
        for j in range(0, 8, 2):
            cj, ck = C[j], C[j+1]
            a, b, d = cj[0][j:j+1], cj[0][j+1:j+2], ck[0][j+1:j+2]
            inv = 1.0 / (a*d - b*b)
            i00, i01, i11 = d*inv, -b*inv, a*inv
            m0 = [x*i00 + y*i01 for x, y in zip(cj, ck)]
            m1 = [x*i01 + y*i11 for x, y in zip(cj, ck)]
            keep = row8 > j+1
            m0[0] = jnp.where(keep, m0[0], 0.0)
            m1[0] = jnp.where(keep, m1[0], 0.0)
            for k in range(j+2, 8):
                p, q = C[k][0][j:j+1], C[k][0][j+1:j+2]
                C[k] = [c - (x*p + y*q) for c, x, y in zip(C[k], m0, m1)]
            p0, q0 = r0[g][j:j+1], r0[g][j+1:j+2]
            p1, q1 = r1[g][j:j+1], r1[g][j+1:j+2]
            done.append((a, b, d, p1, q1))
            for i in range(n):
                if i > 0:
                    r0[g+i] = r0[g+i] - (m0[i]*p0 + m1[i]*q0)
                elif j < 6:
                    r0[g+i] = r0[g+i] - (m0[i]*p0 + m1[i]*q0)
                r1[g+i] = r1[g+i] - (m0[i]*p1 + m1[i]*q1)
    rows = []
    for a, b, d, p1, q1 in done:
        ra = lax.rsqrt(a)
        l10 = b * (1.0 / a)
        rd = lax.rsqrt(d - b*l10)
        rows.append(p1 * ra)
        rows.append((q1 - l10*p1) * rd)
    return jnp.concatenate(rows, axis=0)

def kernel(p_ref, o_ref, s_ref):
    n = 256
    row = lax.broadcasted_iota(jnp.int32, (n, n), 0)
    col = lax.broadcasted_iota(jnp.int32, (n, n), 1)
    eye = (row == col).astype(f32)
    for p in range(2):
        x = p_ref[p]
        g = mm(x, x, ((0,), (0,)), None)
        tr = jnp.sum(g * eye)
        s_ref[p] = g + (0.1 * tr / n + 1e-6) * eye
    for k in range(n // B):
        lo, hi = k*B, (k+1)*B
        t = panel(jnp.concatenate([s_ref[0, lo:hi, lo:hi], s_ref[1, lo:hi, lo:hi]], axis=1))
        for p in range(2):
            w = t[:, p*B:(p+1)*B]
            sk = s_ref[p, lo:hi, :]
            c = lax.broadcasted_iota(jnp.int32, (B, n), 1)
            r = lax.broadcasted_iota(jnp.int32, (B, n), 0)
            sk = jnp.where((c >= lo) & (c < hi), (c - lo == r).astype(f32), sk)
            y = mm(w, sk)
            if hi < n:
                u = mm(s_ref[p, hi:, lo:hi], w, ((1,), (1,)))
                c2 = lax.broadcasted_iota(jnp.int32, (n-hi, n), 1)
                old = jnp.where((c2 >= lo) & (c2 < hi), 0.0, s_ref[p, hi:, :])
                s_ref[p, hi:, :] = old - mm(u, y)
            s_ref[p, lo:hi, :] = y
    for p in range(2):
        w = jnp.where(col <= row, s_ref[p], 0.0)
        w0 = w.astype(jnp.bfloat16)
        e = w - w0.astype(f32)
        w1 = e.astype(jnp.bfloat16)
        w2 = (e - w1.astype(f32)).astype(jnp.bfloat16)
        x = p_ref[p]
        acc = mm(x, w2, ((1,), (1,)), None) + mm(x, w1, ((1,), (1,)), None)
        o_ref[p] = acc + mm(x, w0, ((1,), (1,)), None)

def solve(p):
    return pl.pallas_call(kernel, out_shape=jax.ShapeDtypeStruct((2, 512, 256), f32),
        in_specs=[pl.BlockSpec(memory_space=pltpu.VMEM)], out_specs=pl.BlockSpec(memory_space=pltpu.VMEM),
        scratch_shapes=[pltpu.VMEM((2, 256, 256), f32)],
        compiler_params=pltpu.CompilerParams(vmem_limit_bytes=40 << 20))(p)


def route_whole(buffers, positions):
    arrived = []
    for offset_step in range(buffers.shape[0]):
        arrived.append(
            passed_along(
                (buffers[offset_step], positions[offset_step]), "mesh", offset_step + 1 - FACES
            )
        )
    return (jnp.stack([pair[0] for pair in arrived]), jnp.stack([pair[1] for pair in arrived]))


def body(traces, sketch, face_port, face_pos, tile_count, port_owner):
    slot_count = traces.shape[0]
    face_rows = traces.shape[1]
    partial_sum = jnp.einsum("sfk,kr->sfr", traces, sketch, preferred_element_type=jnp.float32)
    port_total = port_owner.shape[0]
    port_ids = jnp.arange(port_total, dtype=jnp.int32)
    same_owner = port_owner[None, :] == port_owner[:, None]
    rank_table = jnp.sum(
        (same_owner & (port_ids[None, :] < port_ids[:, None])).astype(jnp.int32), axis=1
    )
    port_hit = face_port[:, None] == port_ids[None, :]
    owner_of = jnp.sum(jnp.where(port_hit, port_owner[None, :], 0), axis=1)
    rank_of = jnp.sum(jnp.where(port_hit, rank_table[None, :], 0), axis=1)
    filled = jnp.arange(slot_count, dtype=jnp.int32) < tile_count[0]
    peers = lax.axis_size("mesh")
    my_index = lax.axis_index("mesh")
    spans = FACES + 2
    lowest = 1 - FACES
    distance = (owner_of - my_index - lowest) % peers
    targets = distance * PORT_MOST + rank_of
    selector = (
        (targets[None, :] == jnp.arange(spans * PORT_MOST, dtype=jnp.int32)[:, None])
        & filled[None, :]
    ).astype(jnp.bfloat16)
    send_position = jnp.dot(
        selector, (face_pos + 1).astype(jnp.bfloat16), preferred_element_type=jnp.float32
    ).astype(jnp.bfloat16)
    send_position = send_position.reshape(spans, PORT_MOST)
    owned = jnp.sum((port_owner == my_index).astype(jnp.int32))
    vacant = jnp.arange(PORT_MOST, dtype=jnp.int32) >= owned
    summed = lax.psum(partial_sum, "samp").astype(jnp.bfloat16)
    columns = summed.shape[2]
    placed = jnp.einsum("ts,sfr->tfr", selector, summed, preferred_element_type=jnp.float32).astype(
        jnp.bfloat16
    )
    incoming, position = route_whole(
        placed.reshape(spans, PORT_MOST, face_rows, columns), send_position
    )
    assemble_position = position
    columns = incoming.shape[3]
    assemble_position = assemble_position.T.astype(jnp.float32)
    wanted = (jnp.arange(FACES, dtype=jnp.int32) + 1).astype(jnp.float32)
    chooser = (assemble_position[:, None, :] == wanted[None, :, None]).astype(jnp.bfloat16)
    placed = jnp.einsum("kjs,skfr->kjfr", chooser, incoming, preferred_element_type=jnp.float32)
    port_blocks = placed.astype(jnp.bfloat16).reshape(PORT_MOST, FACES * face_rows, columns)
    return solve(port_blocks)


def solution(mesh):
    placed = (P("mesh", None, "samp"), P("samp", None), P("mesh"), P("mesh"), P("mesh"), P())
    return jax.shard_map(
        body, mesh=mesh, in_specs=placed, out_specs=P("mesh", None, None), check_vma=False
    )
```

```python
import jax
import jax.numpy as jnp
from jax import lax
from jax.experimental import pallas as pl
from jax.experimental.pallas import tpu as pltpu
from jax.sharding import PartitionSpec as P

FACES = 4
QUARTERS = 4
SPAN = 5
B = 64
HI = lax.Precision.HIGHEST
f32 = jnp.float32
bf16 = jnp.bfloat16
VM = pl.BlockSpec(memory_space=pltpu.VMEM)
SM = pl.BlockSpec(memory_space=pltpu.SMEM)
ANY = pl.BlockSpec(memory_space=pl.ANY)
PARAMS = pltpu.CompilerParams(vmem_limit_bytes=40 << 20)
ROUTES = (1, -1, -2, 2, -3)


def shifted(block, axis, distance):
    n = lax.axis_size(axis)
    return lax.ppermute(block, axis, [(i, (i + distance) % n) for i in range(n)])


def mm(a, b, dims=((1,), (0,)), prec=HI):
    return lax.dot_general(a, b, (dims, ((), ())), precision=prec, preferred_element_type=f32)


def sketch_kernel(t_hbm, r_hbm, o0, o1, o2, o3, t, r, sem):
    s = lax.axis_index("samp")
    outs = (o0, o1, o2, o3)
    slots, rows = o0.shape[0], o0.shape[1]
    order = (2, 1, 3, 0)
    load_r = pltpu.make_async_copy(r_hbm, r, sem.at[4])
    load_r.start()
    loads = []
    for k in order:
        c = lax.rem(s + k, QUARTERS)
        load = pltpu.make_async_copy(
            t_hbm.at[:, pl.ds(pl.multiple_of(c * rows, rows), rows), :], t.at[k], sem.at[k]
        )
        load.start()
        loads.append(load)
    load_r.wait()
    for k, load in zip(order, loads):
        load.wait()
        x = t[k].reshape(slots * rows, t.shape[3])
        y = mm(x, r[...], prec=None)
        outs[k][...] = y.reshape(outs[k].shape)


def sketch_parts(traces, sketch):
    slots, cells, samples = traces.shape
    rows = cells // QUARTERS
    rank = sketch.shape[1]
    part = jax.ShapeDtypeStruct((slots, rows, rank), f32)
    return pl.pallas_call(
        sketch_kernel,
        out_shape=[part] * QUARTERS,
        in_specs=[ANY, ANY],
        out_specs=[VM] * QUARTERS,
        scratch_shapes=[
            pltpu.VMEM((QUARTERS, slots, rows, samples), bf16),
            pltpu.VMEM((samples, rank), bf16),
            pltpu.SemaphoreType.DMA((QUARTERS + 1,)),
        ],
        compiler_params=PARAMS,
    )(traces, sketch)


def place_kernel(port, count, owner, a, b, c, d, p1, m1, m2, p2, m3, here, total):
    me = lax.axis_index("mesh")
    n = owner.shape[0]
    total[...] = ((a[...] + b[...]) + (c[...] + d[...])).astype(bf16)
    sends = {}
    for dist in range(SPAN):
        p = lax.rem(me - dist + n, n)
        lean = lax.rem(owner[p] - p + n, n)
        slot = jnp.int32(-1)
        for i in range(total.shape[0]):
            slot = jnp.where((port[i] == p) & (i < count[0]), i, slot)
        sends[dist] = (slot, lean)

    def tile(dist, lean):
        slot, its = sends[dist]
        good = (slot >= 0) & (its == lean)
        return jnp.where(good, total[jnp.maximum(slot, 0)], jnp.inf).astype(bf16)

    for out, near in ((p1, 0), (here, 1), (m1, 2), (m2, 3)):
        out[0] = tile(near, 1)
        out[1] = tile(near + 1, 2)
    p2[0] = tile(0, 2)
    m3[0] = tile(4, 1)


def place(face_port, tile_count, port_owner, parts):
    slots, rows, rank = parts[0].shape
    two = jax.ShapeDtypeStruct((2, rows, rank), bf16)
    one = jax.ShapeDtypeStruct((1, rows, rank), bf16)
    return pl.pallas_call(
        place_kernel,
        out_shape=[two, two, two, one, one, two],
        in_specs=[SM] * 3 + [VM] * 4,
        out_specs=[VM] * 6,
        scratch_shapes=[pltpu.VMEM((slots, rows, rank), bf16)],
        compiler_params=PARAMS,
    )(face_port, tile_count, port_owner, *parts)


def pick_kernel(p1, m1, m2, p2, m3, here, out):
    near = [p1[0], here[0], m1[0], m2[0], m3[0]]
    far = [p2[0], p1[1], here[1], m1[1], m2[1]]
    for lean, tiles in enumerate((near, far)):
        tiles = [t.astype(f32) for t in tiles]
        full = [t < jnp.inf for t in tiles]
        run = full[0]
        for j in range(FACES):
            if j:
                run = run & full[j]
            x = jnp.where(run, tiles[j], tiles[j + 1])
            out[lean, j] = jnp.where(x < jnp.inf, x, 0.0).astype(bf16)


def pick(tiles):
    rows, rank = tiles[0].shape[1:]
    return pl.pallas_call(
        pick_kernel,
        out_shape=jax.ShapeDtypeStruct((2, FACES, rows, rank), bf16),
        in_specs=[VM] * 6,
        out_specs=VM,
        compiler_params=PARAMS,
    )(*tiles)


def panel(t0):
    lane = lax.broadcasted_iota(jnp.int32, (B, 128), 1)
    row = lax.broadcasted_iota(jnp.int32, (B, 128), 0)
    t1 = ((lane % B) == row).astype(f32)
    half = jnp.where(lane < B, 0, B)
    groups = B // 8
    r0 = [t0[8 * i : 8 * i + 8] for i in range(groups)]
    r1 = [t1[8 * i : 8 * i + 8] for i in range(groups)]
    h8, row8 = half[:8], row[:8]
    done = []
    for g in range(groups):
        n = groups - g
        cols = [
            [
                jnp.take_along_axis(r0[g + i], h8 + (8 * g + j), axis=1, mode="promise_in_bounds")
                for i in range(n)
            ]
            for j in range(8)
        ]
        for j in range(0, 8, 2):
            cj, ck = cols[j], cols[j + 1]
            a, b, d = cj[0][j : j + 1], cj[0][j + 1 : j + 2], ck[0][j + 1 : j + 2]
            inv = 1.0 / (a * d - b * b)
            i00, i01, i11 = d * inv, -b * inv, a * inv
            m0 = [x * i00 + y * i01 for x, y in zip(cj, ck)]
            m1 = [x * i01 + y * i11 for x, y in zip(cj, ck)]
            keep = row8 > j + 1
            m0[0] = jnp.where(keep, m0[0], 0.0)
            m1[0] = jnp.where(keep, m1[0], 0.0)
            for k in range(j + 2, 8):
                p, q = cols[k][0][j : j + 1], cols[k][0][j + 1 : j + 2]
                cols[k] = [c - (x * p + y * q) for c, x, y in zip(cols[k], m0, m1)]
            p0, q0 = r0[g][j : j + 1], r0[g][j + 1 : j + 2]
            p1, q1 = r1[g][j : j + 1], r1[g][j + 1 : j + 2]
            done.append((a, b, d, p1, q1))
            for i in range(n):
                if i > 0 or j < 6:
                    r0[g + i] = r0[g + i] - (m0[i] * p0 + m1[i] * q0)
                r1[g + i] = r1[g + i] - (m0[i] * p1 + m1[i] * q1)
    rows = []
    for a, b, d, p1, q1 in done:
        l10 = b * (1.0 / a)
        rows.append(p1 * lax.rsqrt(a))
        rows.append((q1 - l10 * p1) * lax.rsqrt(d - b * l10))
    return jnp.concatenate(rows, axis=0)


def solve_kernel(owner, x0, x1, x2, x3, o_ref, x_ref, s_ref):
    me = lax.axis_index("mesh")
    s = lax.axis_index("samp")
    ports = owner.shape[0]
    near, far = lax.rem(me - 1 + ports, ports), lax.rem(me - 2 + ports, ports)
    both = (owner[near] == me) & (owner[far] == me)
    near_first = jnp.where(both, near < far, owner[near] == me)
    slots = (jnp.where(near_first, 0, 1), jnp.where(near_first, 1, 0))
    n = x0.shape[3]
    rows = x0.shape[2]
    each = FACES * rows
    row = lax.broadcasted_iota(jnp.int32, (n, n), 0)
    col = lax.broadcasted_iota(jnp.int32, (n, n), 1)
    eye = (row == col).astype(f32)
    for p in range(2):
        for k, x in enumerate((x0, x1, x2, x3)):
            x_ref[p, k * each : (k + 1) * each] = x[p].reshape(each, n)
        x = x_ref[p]
        g = mm(x, x, ((0,), (0,)), None)
        s_ref[p] = g + (0.1 * jnp.sum(g * eye) / n + 1e-6) * eye
    for k in range(n // B):
        lo, hi = k * B, (k + 1) * B
        t = panel(jnp.concatenate([s_ref[0, lo:hi, lo:hi], s_ref[1, lo:hi, lo:hi]], axis=1))
        for p in range(2):
            w = t[:, p * B : (p + 1) * B]
            c = col[:B]
            inside = (c >= lo) & (c < hi)
            sk = jnp.where(inside, (c - lo == row[:B]).astype(f32), s_ref[p, lo:hi, :])
            y = mm(w, sk)
            if hi < n:
                u = mm(s_ref[p, hi:, lo:hi], w, ((1,), (1,)))
                c = col[hi:]
                old = jnp.where((c >= lo) & (c < hi), 0.0, s_ref[p, hi:, :])
                s_ref[p, hi:, :] = old - mm(u, y)
            s_ref[p, lo:hi, :] = y
    for p in range(2):
        w = jnp.where(col <= row, s_ref[p], 0.0)
        w0 = w.astype(bf16)
        e = w - w0.astype(f32)
        w1 = e.astype(bf16)
        w2 = (e - w1.astype(f32)).astype(bf16)
        x = x_ref[p]
        acc = mm(x, w2, ((1,), (1,)), None) + mm(x, w1, ((1,), (1,)), None)
        y = acc + mm(x, w0, ((1,), (1,)), None)
        for k in range(QUARTERS):
            q = lax.rem(s - k + QUARTERS, QUARTERS)
            for j in range(FACES):
                at = pl.multiple_of(j * QUARTERS * rows + q * rows, rows)
                o_ref[slots[p], pl.ds(at, rows), :] = y[k * each + j * rows : k * each + (j + 1) * rows]


def solve(port_owner, pieces):
    rows, n = pieces[0].shape[2:]
    height = FACES * QUARTERS * rows
    return pl.pallas_call(
        solve_kernel,
        out_shape=jax.ShapeDtypeStruct((2, height, n), f32),
        in_specs=[SM] + [VM] * QUARTERS,
        out_specs=VM,
        scratch_shapes=[pltpu.VMEM((2, height, n), bf16), pltpu.VMEM((2, n, n), f32)],
        compiler_params=PARAMS,
    )(port_owner, *pieces)


def body(traces, sketch, face_port, face_pos, tile_count, port_owner):
    own, k1, k2, k3 = sketch_parts(traces, sketch)
    k2 = shifted(k2, "samp", 2)
    k1 = shifted(k1, "samp", 1)
    k3 = shifted(k3, "samp", -1)
    *sends, here = place(face_port, tile_count, port_owner, (own, k1, k2, k3))
    tiles = [shifted(x, "mesh", distance) for x, distance in zip(sends, ROUTES)]
    mine = pick((*tiles, here))
    pieces = [mine] + [shifted(mine, "samp", k) for k in range(1, QUARTERS)]
    return solve(port_owner, pieces)


def solution(mesh):
    placed = (P("mesh", None, "samp"), P("samp", None), P("mesh"), P("mesh"), P("mesh"), P())
    return jax.shard_map(
        body, mesh=mesh, in_specs=placed, out_specs=P("mesh", None, None), check_vma=False
    )
```

```python
import jax
import jax.numpy as jnp
from jax import lax
from jax.experimental import pallas as pl
from jax.experimental.pallas import tpu as pltpu
from jax.sharding import PartitionSpec as P

FACES = 4
QUARTERS = 4
SPAN = 5
B = 64
HI = lax.Precision.HIGHEST
f32 = jnp.float32
bf16 = jnp.bfloat16
VM = pl.BlockSpec(memory_space=pltpu.VMEM)
SM = pl.BlockSpec(memory_space=pltpu.SMEM)
ANY = pl.BlockSpec(memory_space=pltpu.HBM)
PARAMS = pltpu.CompilerParams(vmem_limit_bytes=24 << 20)
WIDE = pltpu.CompilerParams(vmem_limit_bytes=54300 << 10)
ROUTES = (1, -1, -2, 2, -3)


def shifted(block, axis, distance):
    n = lax.axis_size(axis)
    return lax.ppermute(block, axis, [(i, (i + distance) % n) for i in range(n)])


def mm(a, b, dims=((1,), (0,)), prec=HI):
    return lax.dot_general(a, b, (dims, ((), ())), precision=prec, preferred_element_type=f32)


def sketch_kernel(t_hbm, r_hbm, o0, o1, o2, o3, t, r, sem):
    s = lax.axis_index("samp")
    outs = (o0, o1, o2, o3)
    slots, rows = o0.shape[0], o0.shape[1]
    order = (2, 1, 3, 0)
    load_r = pltpu.make_async_copy(r_hbm, r, sem.at[4])
    load_r.start()
    loads = []
    for k in order:
        c = lax.rem(s + k, QUARTERS)
        load = pltpu.make_async_copy(
            t_hbm.at[:, pl.ds(pl.multiple_of(c * rows, rows), rows), :], t.at[k], sem.at[k]
        )
        load.start()
        loads.append(load)
    load_r.wait()
    for k, load in zip(order, loads):
        load.wait()
        x = t[k].reshape(slots * rows, t.shape[3])
        y = mm(x, r[...], prec=None)
        outs[k][...] = y.reshape(outs[k].shape)


def sketch_parts(traces, sketch):
    slots, cells, samples = traces.shape
    rows = cells // QUARTERS
    rank = sketch.shape[1]
    part = jax.ShapeDtypeStruct((slots, rows, rank), f32)
    return pl.pallas_call(
        sketch_kernel,
        out_shape=[part] * QUARTERS,
        in_specs=[ANY, ANY],
        out_specs=[VM] * QUARTERS,
        scratch_shapes=[
            pltpu.VMEM((QUARTERS, slots, rows, samples), bf16),
            pltpu.VMEM((samples, rank), bf16),
            pltpu.SemaphoreType.DMA((QUARTERS + 1,)),
        ],
        compiler_params=WIDE,
    )(traces, sketch)


def place_kernel(port, count, owner, a, b, c, d, p1, m1, m2, p2, m3, here, total):
    me = lax.axis_index("mesh")
    n = owner.shape[0]
    total[...] = ((a[...] + b[...]) + (c[...] + d[...])).astype(bf16)
    sends = {}
    for dist in range(SPAN):
        p = lax.rem(me - dist + n, n)
        lean = lax.rem(owner[p] - p + n, n)
        slot = jnp.int32(-1)
        for i in range(total.shape[0]):
            slot = jnp.where((port[i] == p) & (i < count[0]), i, slot)
        sends[dist] = (slot, lean)

    def tile(dist, lean):
        slot, its = sends[dist]
        good = (slot >= 0) & (its == lean)
        return jnp.where(good, total[jnp.maximum(slot, 0)], jnp.inf).astype(bf16)

    for out, near in ((p1, 0), (here, 1), (m1, 2), (m2, 3)):
        out[0] = tile(near, 1)
        out[1] = tile(near + 1, 2)
    p2[0] = tile(0, 2)
    m3[0] = tile(4, 1)


def place(face_port, tile_count, port_owner, parts):
    slots, rows, rank = parts[0].shape
    two = jax.ShapeDtypeStruct((2, rows, rank), bf16)
    one = jax.ShapeDtypeStruct((1, rows, rank), bf16)
    return pl.pallas_call(
        place_kernel,
        out_shape=[two, two, two, one, one, two],
        in_specs=[SM] * 3 + [VM] * 4,
        out_specs=[VM] * 6,
        scratch_shapes=[pltpu.VMEM((slots, rows, rank), bf16)],
        compiler_params=PARAMS,
    )(face_port, tile_count, port_owner, *parts)


def pick_kernel(p1, m1, m2, p2, m3, here, out):
    near = [p1[0], here[0], m1[0], m2[0], m3[0]]
    far = [p2[0], p1[1], here[1], m1[1], m2[1]]
    for lean, tiles in enumerate((near, far)):
        tiles = [t.astype(f32) for t in tiles]
        full = [t < jnp.inf for t in tiles]
        run = full[0]
        for j in range(FACES):
            if j:
                run = run & full[j]
            x = jnp.where(run, tiles[j], tiles[j + 1])
            out[lean, j] = jnp.where(x < jnp.inf, x, 0.0).astype(bf16)


def pick(tiles):
    rows, rank = tiles[0].shape[1:]
    return pl.pallas_call(
        pick_kernel,
        out_shape=jax.ShapeDtypeStruct((2, FACES, rows, rank), bf16),
        in_specs=[VM] * 6,
        out_specs=VM,
        compiler_params=PARAMS,
    )(*tiles)


def panel(t0):
    lane = lax.broadcasted_iota(jnp.int32, (B, 128), 1)
    row = lax.broadcasted_iota(jnp.int32, (B, 128), 0)
    t1 = ((lane % B) == row).astype(f32)
    groups = B // 8
    r0 = [t0[8 * i : 8 * i + 8] for i in range(groups)]
    r1 = [t1[8 * i : 8 * i + 8] for i in range(groups)]
    half, row8 = jnp.where(lane < B, 0, B)[:8], row[:8]

    def column(block, c):
        return jnp.take_along_axis(block, half + c, axis=1, mode="promise_in_bounds")

    done = []
    ahead = [[column(r0[0], j)] for j in range(8)]
    for g in range(groups):
        n = groups - g
        cur = [
            [ahead[j][-1]] + [column(r0[g + i], 8 * g + j) for i in range(1, n)] for j in range(8)
        ]
        ahead = []
        if n > 1:
            ahead = [[column(r0[g + i], 8 * g + 8 + j) for i in range(2)] for j in range(8)]
        for j in range(0, 8, 2):
            cj, ck = cur[j], cur[j + 1]
            a, b, d = cj[0][j : j + 1], cj[0][j + 1 : j + 2], ck[0][j + 1 : j + 2]
            det = a * d - b * b
            inv = pl.reciprocal(det, approx=True)
            inv = inv * (2.0 - det * inv)
            m0 = [x * d - y * b for x, y in zip(cj, ck)]
            m1 = [y * a - x * b for x, y in zip(cj, ck)]
            m0[0] = jnp.where(row8 > j + 1, m0[0], 0.0)
            m1[0] = jnp.where(row8 > j + 1, m1[0], 0.0)

            def swept(top, blocks):
                p, q = top[j : j + 1] * inv, top[j + 1 : j + 2] * inv
                return [c - (x * p + y * q) for c, x, y in zip(blocks, m0, m1)]

            for k in range(j + 2, 8):
                cur[k] = swept(cur[k][0], cur[k])
            ahead = [swept(c[0], c) for c in ahead]
            done.append((a, b, d, r1[g][j : j + 1], r1[g][j + 1 : j + 2]))
            r0[g:] = swept(r0[g], r0[g:])
            r1[g:] = swept(r1[g], r1[g:])
    rows = []
    for a, b, d, p1, q1 in done:
        l10 = b * (1.0 / a)
        rows.append(p1 * lax.rsqrt(a))
        rows.append((q1 - l10 * p1) * lax.rsqrt(d - b * l10))
    return jnp.concatenate(rows, axis=0)


def solve_kernel(owner, x0, x1, x2, x3, o_hbm, x_ref, o_ref, sem):
    me = lax.axis_index("mesh")
    s = lax.axis_index("samp")
    ports = owner.shape[0]
    near, far = lax.rem(me - 1 + ports, ports), lax.rem(me - 2 + ports, ports)
    both = (owner[near] == me) & (owner[far] == me)
    near_first = jnp.where(both, near < far, owner[near] == me)
    slots = (jnp.where(near_first, 0, 1), jnp.where(near_first, 1, 0))
    n = x0.shape[3]
    rows = x0.shape[2]
    each = FACES * rows
    row = lax.broadcasted_iota(jnp.int32, (n, n), 0)
    col = lax.broadcasted_iota(jnp.int32, (n, n), 1)
    eye = (row == col).astype(f32)
    blocks = []
    for p in range(2):
        for k, x in enumerate((x0, x1, x2, x3)):
            x_ref[p, k * each : (k + 1) * each] = x[p].reshape(each, n)
        x = x_ref[p]
        g = mm(x, x, ((0,), (0,)), None)
        g = g + (0.1 * jnp.sum(g * eye) / n + 1e-6) * eye
        blocks.append([g[k * B : (k + 1) * B] for k in range(n // B)])
    col, row = col[:B], row[:B]
    for k in range(n // B):
        lo, hi = k * B, (k + 1) * B
        inside = (col >= lo) & (col < hi)
        t = panel(jnp.concatenate([s[k][:, lo:hi] for s in blocks], axis=1))
        ys = []
        for p in range(2):
            w = t[:, p * B : (p + 1) * B]
            sk = jnp.where(inside, (col - lo == row).astype(f32), blocks[p][k])
            blocks[p][k] = mm(w, sk)
            ys.append(w)
        for i in range(k + 1, n // B):
            for p in range(2):
                u = mm(blocks[p][i][:, lo:hi], ys[p], ((1,), (1,)))
                blocks[p][i] = jnp.where(inside, 0.0, blocks[p][i]) - mm(u, blocks[p][k])
    stores = []
    for p in range(2):
        w = [jnp.where(col <= row + k * B, s, 0.0) for k, s in enumerate(blocks[p])]
        w = jnp.concatenate(w, axis=0)
        w0 = w.astype(bf16)
        e = w - w0.astype(f32)
        w1 = e.astype(bf16)
        w2 = (e - w1.astype(f32)).astype(bf16)
        x = x_ref[p]
        acc = mm(x, w2, ((1,), (1,)), None) + mm(x, w1, ((1,), (1,)), None)
        y = acc + mm(x, w0, ((1,), (1,)), None)
        for k in range(QUARTERS):
            q = lax.rem(s - k + QUARTERS, QUARTERS)
            for j in range(FACES):
                at = pl.multiple_of(j * QUARTERS * rows + q * rows, rows)
                o_ref[p, pl.ds(at, rows), :] = y[k * each + j * rows : k * each + (j + 1) * rows]
        store = pltpu.make_async_copy(o_ref.at[p], o_hbm.at[slots[p]], sem.at[p])
        store.start()
        stores.append(store)
    for store in stores:
        store.wait()


def solve(port_owner, pieces):
    rows, n = pieces[0].shape[2:]
    height = FACES * QUARTERS * rows
    return pl.pallas_call(
        solve_kernel,
        out_shape=jax.ShapeDtypeStruct((2, height, n), f32),
        in_specs=[SM] + [VM] * QUARTERS,
        out_specs=ANY,
        scratch_shapes=[
            pltpu.VMEM((2, height, n), bf16),
            pltpu.VMEM((2, height, n), f32),
            pltpu.SemaphoreType.DMA((2,)),
        ],
        compiler_params=PARAMS,
    )(port_owner, *pieces)


def body(traces, sketch, face_port, face_pos, tile_count, port_owner):
    own, k1, k2, k3 = sketch_parts(traces, sketch)
    k2 = shifted(k2, "samp", 2)
    k1 = shifted(k1, "samp", 1)
    k3 = shifted(k3, "samp", -1)
    *sends, here = place(face_port, tile_count, port_owner, (own, k1, k2, k3))
    tiles = [shifted(x, "mesh", distance) for x, distance in zip(sends, ROUTES)]
    mine = pick((*tiles, here))
    pieces = [mine] + [shifted(mine, "samp", k) for k in range(1, QUARTERS)]
    return solve(port_owner, pieces)


def solution(mesh):
    placed = (P("mesh", None, "samp"), P("samp", None), P("mesh"), P("mesh"), P("mesh"), P())
    return jax.shard_map(
        body, mesh=mesh, in_specs=placed, out_specs=P("mesh", None, None), check_vma=False
    )
```

```python
import functools

import jax
import jax.numpy as jnp
from jax import lax
from jax.experimental import pallas as pl
from jax.experimental.pallas import tpu as pltpu
from jax.sharding import PartitionSpec as P

FACES = 4
QUARTERS = 4
SPAN = 5
B = 64
HI = lax.Precision.HIGHEST
f32 = jnp.float32
bf16 = jnp.bfloat16
VM = pl.BlockSpec(memory_space=pltpu.VMEM)
SM = pl.BlockSpec(memory_space=pltpu.SMEM)
ANY = pl.BlockSpec(memory_space=pltpu.HBM)
PARAMS = pltpu.CompilerParams(vmem_limit_bytes=24 << 20)
WIDE = pltpu.CompilerParams(vmem_limit_bytes=54300 << 10)
TURNS = (0, 2, 1, 3)
ROUTES = (2, -2, -3, 1, -1)


def shifted(block, axis, distance):
    n = lax.axis_size(axis)
    return lax.ppermute(block, axis, [(i, (i + distance) % n) for i in range(n)])


def mm(a, b, dims=((1,), (0,)), prec=HI):
    return lax.dot_general(a, b, (dims, ((), ())), precision=prec, preferred_element_type=f32)


def sketch_kernel(turns, t_hbm, r_hbm, *refs):
    outs, (t, r, sem) = refs[: len(turns)], refs[len(turns) :]
    s = lax.axis_index("samp")
    slots, rows = outs[0].shape[:2]
    load_r = pltpu.make_async_copy(r_hbm, r, sem.at[len(turns)])
    load_r.start()
    loads = []
    for i, k in enumerate(turns):
        c = lax.rem(s + k, QUARTERS)
        load = pltpu.make_async_copy(
            t_hbm.at[:, pl.ds(pl.multiple_of(c * rows, rows), rows), :], t.at[i], sem.at[i]
        )
        load.start()
        loads.append(load)
    load_r.wait()
    for i, load in enumerate(loads):
        load.wait()
        y = mm(t[i].reshape(slots * rows, t.shape[3]), r[...], prec=None)
        outs[i][...] = y.reshape(outs[i].shape)


def sketch_parts(traces, sketch, turns):
    slots, cells, samples = traces.shape
    rows = cells // QUARTERS
    rank = sketch.shape[1]
    part = jax.ShapeDtypeStruct((slots, rows, rank), f32)
    return pl.pallas_call(
        functools.partial(sketch_kernel, turns),
        out_shape=[part] * len(turns),
        in_specs=[ANY, ANY],
        out_specs=[VM] * len(turns),
        scratch_shapes=[
            pltpu.VMEM((len(turns), slots, rows, samples), bf16),
            pltpu.VMEM((samples, rank), bf16),
            pltpu.SemaphoreType.DMA((len(turns) + 1,)),
        ],
        compiler_params=WIDE,
    )(traces, sketch)


def place_kernel(port, count, owner, a, b, c, d, p2, m2, m3, p1, m1, here, total):
    me = lax.axis_index("mesh")
    n = owner.shape[0]
    total[...] = ((a[...] + b[...]) + (c[...] + d[...])).astype(bf16)
    sends = {}
    for dist in range(SPAN):
        p = lax.rem(me - dist + n, n)
        lean = lax.rem(owner[p] - p + n, n)
        slot = jnp.int32(-1)
        for i in range(total.shape[0]):
            slot = jnp.where((port[i] == p) & (i < count[0]), i, slot)
        sends[dist] = (slot, lean)

    def tile(dist, lean):
        slot, its = sends[dist]
        good = (slot >= 0) & (its == lean)
        return jnp.where(good, total[jnp.maximum(slot, 0)], jnp.inf).astype(bf16)

    for out, near in ((p1, 0), (here, 1), (m1, 2), (m2, 3)):
        out[0] = tile(near, 1)
        out[1] = tile(near + 1, 2)
    p2[0] = tile(0, 2)
    m3[0] = tile(4, 1)
    p2[1] = p2[0]
    m3[1] = m3[0]


def place(face_port, tile_count, port_owner, parts):
    slots, rows, rank = parts[0].shape
    two = jax.ShapeDtypeStruct((2, rows, rank), bf16)
    return pl.pallas_call(
        place_kernel,
        out_shape=[two] * 6,
        in_specs=[SM] * 3 + [VM] * 4,
        out_specs=[VM] * 6,
        scratch_shapes=[pltpu.VMEM((slots, rows, rank), bf16)],
        compiler_params=PARAMS,
    )(face_port, tile_count, port_owner, *parts)


def pick_kernel(p2, m2, m3, p1, m1, here, out):
    near = [p1[0], here[0], m1[0], m2[0], m3[0]]
    far = [p2[0], p1[1], here[1], m1[1], m2[1]]
    for lean, tiles in enumerate((near, far)):
        tiles = [t.astype(f32) for t in tiles]
        full = [t < jnp.inf for t in tiles]
        run = full[0]
        for j in range(FACES):
            if j:
                run = run & full[j]
            x = jnp.where(run, tiles[j], tiles[j + 1])
            out[lean, j] = jnp.where(x < jnp.inf, x, 0.0).astype(bf16)


def pick(tiles):
    rows, rank = tiles[0].shape[1:]
    return pl.pallas_call(
        pick_kernel,
        out_shape=jax.ShapeDtypeStruct((2, FACES, rows, rank), bf16),
        in_specs=[VM] * 6,
        out_specs=VM,
        compiler_params=PARAMS,
    )(*tiles)


def panel(t0):
    lane = lax.broadcasted_iota(jnp.int32, (B, 128), 1)
    row = lax.broadcasted_iota(jnp.int32, (B, 128), 0)
    t1 = ((lane % B) == row).astype(f32)
    groups = B // 8
    r0 = [t0[8 * i : 8 * i + 8] for i in range(groups)]
    r1 = [t1[8 * i : 8 * i + 8] for i in range(groups)]
    half, row8 = jnp.where(lane < B, 0, B)[:8], row[:8]

    def column(block, c):
        return jnp.take_along_axis(block, half + c, axis=1, mode="promise_in_bounds")

    done = []
    ahead = [[column(r0[0], j)] for j in range(8)]
    for g in range(groups):
        n = groups - g
        cur = [
            [ahead[j][-1]] + [column(r0[g + i], 8 * g + j) for i in range(1, n)] for j in range(8)
        ]
        ahead = []
        if n > 1:
            ahead = [[column(r0[g + i], 8 * g + 8 + j) for i in range(2)] for j in range(8)]
        for j in range(0, 8, 2):
            cj, ck = cur[j], cur[j + 1]
            a, b, d = cj[0][j : j + 1], cj[0][j + 1 : j + 2], ck[0][j + 1 : j + 2]
            det = a * d - b * b
            inv = pl.reciprocal(det, approx=True)
            inv = inv * (2.0 - det * inv)
            m0 = [x * d - y * b for x, y in zip(cj, ck)]
            m1 = [y * a - x * b for x, y in zip(cj, ck)]
            m0[0] = jnp.where(row8 > j + 1, m0[0], 0.0)
            m1[0] = jnp.where(row8 > j + 1, m1[0], 0.0)

            def swept(top, blocks):
                p, q = top[j : j + 1] * inv, top[j + 1 : j + 2] * inv
                return [c - (x * p + y * q) for c, x, y in zip(blocks, m0, m1)]

            for k in range(j + 2, 8):
                cur[k] = swept(cur[k][0], cur[k])
            ahead = [swept(c[0], c) for c in ahead]
            done.append((a, b, d, r1[g][j : j + 1], r1[g][j + 1 : j + 2]))
            r0[g:] = swept(r0[g], r0[g:])
            r1[g:] = swept(r1[g], r1[g:])
    rows = []
    for a, b, d, p1, q1 in done:
        l10 = b * (1.0 / a)
        rows.append(p1 * lax.rsqrt(a))
        rows.append((q1 - l10 * p1) * lax.rsqrt(d - b * l10))
    return jnp.concatenate(rows, axis=0)


def solve_kernel(owner, x0, x1, x2, x3, o_hbm, x_ref, o_ref, sem):
    me = lax.axis_index("mesh")
    s = lax.axis_index("samp")
    ports = owner.shape[0]
    near, far = lax.rem(me - 1 + ports, ports), lax.rem(me - 2 + ports, ports)
    both = (owner[near] == me) & (owner[far] == me)
    near_first = jnp.where(both, near < far, owner[near] == me)
    slots = (jnp.where(near_first, 0, 1), jnp.where(near_first, 1, 0))
    n = x0.shape[3]
    rows = x0.shape[2]
    each = FACES * rows
    row = lax.broadcasted_iota(jnp.int32, (n, n), 0)
    col = lax.broadcasted_iota(jnp.int32, (n, n), 1)
    eye = (row == col).astype(f32)
    blocks = []
    for p in range(2):
        for k, x in enumerate((x0, x1, x2, x3)):
            x_ref[p, k * each : (k + 1) * each] = x[p].reshape(each, n)
        x = x_ref[p]
        g = mm(x, x, ((0,), (0,)), None)
        g = g + (0.1 * jnp.sum(g * eye) / n + 1e-6) * eye
        blocks.append([g[k * B : (k + 1) * B] for k in range(n // B)])
    col, row = col[:B], row[:B]
    for k in range(n // B):
        lo, hi = k * B, (k + 1) * B
        inside = (col >= lo) & (col < hi)
        t = panel(jnp.concatenate([s[k][:, lo:hi] for s in blocks], axis=1))
        ys = []
        for p in range(2):
            w = t[:, p * B : (p + 1) * B]
            sk = jnp.where(inside, (col - lo == row).astype(f32), blocks[p][k])
            blocks[p][k] = mm(w, sk)
            ys.append(w)
        for i in range(k + 1, n // B):
            for p in range(2):
                u = mm(blocks[p][i][:, lo:hi], ys[p], ((1,), (1,)))
                blocks[p][i] = jnp.where(inside, 0.0, blocks[p][i]) - mm(u, blocks[p][k])
    stores = []
    for p in range(2):
        w = [jnp.where(col <= row + k * B, s, 0.0) for k, s in enumerate(blocks[p])]
        w = jnp.concatenate(w, axis=0)
        w0 = w.astype(bf16)
        e = w - w0.astype(f32)
        w1 = e.astype(bf16)
        w2 = (e - w1.astype(f32)).astype(bf16)
        x = x_ref[p]
        acc = mm(x, w2, ((1,), (1,)), None) + mm(x, w1, ((1,), (1,)), None)
        y = acc + mm(x, w0, ((1,), (1,)), None)
        for k in range(QUARTERS):
            q = lax.rem(s - TURNS[k] + QUARTERS, QUARTERS)
            for j in range(FACES):
                at = pl.multiple_of(j * QUARTERS * rows + q * rows, rows)
                o_ref[p, pl.ds(at, rows), :] = y[k * each + j * rows : k * each + (j + 1) * rows]
        store = pltpu.make_async_copy(o_ref.at[p], o_hbm.at[slots[p]], sem.at[p])
        store.start()
        stores.append(store)
    for store in stores:
        store.wait()


def solve(port_owner, pieces):
    rows, n = pieces[0].shape[2:]
    height = FACES * QUARTERS * rows
    return pl.pallas_call(
        solve_kernel,
        out_shape=jax.ShapeDtypeStruct((2, height, n), f32),
        in_specs=[SM] + [VM] * QUARTERS,
        out_specs=ANY,
        scratch_shapes=[
            pltpu.VMEM((2, height, n), bf16),
            pltpu.VMEM((2, height, n), f32),
            pltpu.SemaphoreType.DMA((2,)),
        ],
        compiler_params=PARAMS,
    )(port_owner, *pieces)


def body(traces, sketch, face_port, face_pos, tile_count, port_owner):
    (k2,) = sketch_parts(traces, sketch, (2,))
    k1, k3, own = sketch_parts(traces, sketch, (1, 3, 0))
    k2 = shifted(k2, "samp", 2)
    k1 = shifted(k1, "samp", 1)
    k3 = shifted(k3, "samp", -1)
    *sends, here = place(face_port, tile_count, port_owner, (own, k1, k2, k3))
    tiles = [shifted(x, "mesh", distance) for x, distance in zip(sends, ROUTES)]
    mine = pick((*tiles, here))
    pieces = [mine] + [shifted(mine, "samp", k) for k in TURNS[1:]]
    return solve(port_owner, pieces)


def solution(mesh):
    placed = (P("mesh", None, "samp"), P("samp", None), P("mesh"), P("mesh"), P("mesh"), P())
    return jax.shard_map(
        body, mesh=mesh, in_specs=placed, out_specs=P("mesh", None, None), check_vma=False
    )
```

```python
import functools

import jax
import jax.numpy as jnp
from jax import lax
from jax.experimental import pallas as pl
from jax.experimental.pallas import tpu as pltpu
from jax.sharding import PartitionSpec as P

FACES = 4
QUARTERS = 4
SPAN = 5
B = 64
HI = lax.Precision.HIGHEST
f32 = jnp.float32
bf16 = jnp.bfloat16
VM = pl.BlockSpec(memory_space=pltpu.VMEM)
SM = pl.BlockSpec(memory_space=pltpu.SMEM)
ANY = pl.BlockSpec(memory_space=pltpu.HBM)
PARAMS = pltpu.CompilerParams(vmem_limit_bytes=24 << 20)
WIDE = pltpu.CompilerParams(vmem_limit_bytes=54300 << 10)
TURNS = (0, 3, 1, 2)
ROUTES = (2, -2, -3, 1, -1)


def shifted(block, axis, distance):
    n = lax.axis_size(axis)
    return lax.ppermute(block, axis, [(i, (i + distance) % n) for i in range(n)])


def mm(a, b, dims=((1,), (0,)), prec=HI):
    return lax.dot_general(a, b, (dims, ((), ())), precision=prec, preferred_element_type=f32)


def sketch_kernel(turns, t_hbm, r_hbm, *refs):
    outs, (t, r, sem) = refs[: len(turns)], refs[len(turns) :]
    s = lax.axis_index("samp")
    slots, rows = outs[0].shape[:2]
    load_r = pltpu.make_async_copy(r_hbm, r, sem.at[len(turns)])
    load_r.start()
    loads = []
    for i, k in enumerate(turns):
        c = lax.rem(s + k, QUARTERS)
        load = pltpu.make_async_copy(
            t_hbm.at[:, pl.ds(pl.multiple_of(c * rows, rows), rows), :], t.at[i], sem.at[i]
        )
        load.start()
        loads.append(load)
    load_r.wait()
    for i, load in enumerate(loads):
        load.wait()
        y = mm(t[i].reshape(slots * rows, t.shape[3]), r[...], prec=None)
        outs[i][...] = y.reshape(outs[i].shape)


def sketch_parts(traces, sketch, turns):
    slots, cells, samples = traces.shape
    rows = cells // QUARTERS
    rank = sketch.shape[1]
    part = jax.ShapeDtypeStruct((slots, rows, rank), f32)
    return pl.pallas_call(
        functools.partial(sketch_kernel, turns),
        out_shape=[part] * len(turns),
        in_specs=[ANY, ANY],
        out_specs=[VM] * len(turns),
        scratch_shapes=[
            pltpu.VMEM((len(turns), slots, rows, samples), bf16),
            pltpu.VMEM((samples, rank), bf16),
            pltpu.SemaphoreType.DMA((len(turns) + 1,)),
        ],
        compiler_params=WIDE,
    )(traces, sketch)


def place_kernel(port, count, owner, a, b, c, d, p2, m2, m3, p1, m1, here, total):
    me = lax.axis_index("mesh")
    n = owner.shape[0]
    total[...] = ((a[...] + b[...]) + (c[...] + d[...])).astype(bf16)
    sends = {}
    for dist in range(SPAN):
        p = lax.rem(me - dist + n, n)
        lean = lax.rem(owner[p] - p + n, n)
        slot = jnp.int32(-1)
        for i in range(total.shape[0]):
            slot = jnp.where((port[i] == p) & (i < count[0]), i, slot)
        sends[dist] = (slot, lean)

    def tile(dist, lean):
        slot, its = sends[dist]
        good = (slot >= 0) & (its == lean)
        return jnp.where(good, total[jnp.maximum(slot, 0)], jnp.inf).astype(bf16)

    for out, near in ((p1, 0), (here, 1), (m1, 2), (m2, 3)):
        out[0] = tile(near, 1)
        out[1] = tile(near + 1, 2)
    p2[0] = tile(0, 2)
    m3[0] = tile(4, 1)
    p2[1] = p2[0]
    m3[1] = m3[0]


def place(face_port, tile_count, port_owner, parts):
    slots, rows, rank = parts[0].shape
    two = jax.ShapeDtypeStruct((2, rows, rank), bf16)
    return pl.pallas_call(
        place_kernel,
        out_shape=[two] * 6,
        in_specs=[SM] * 3 + [VM] * 4,
        out_specs=[VM] * 6,
        scratch_shapes=[pltpu.VMEM((slots, rows, rank), bf16)],
        compiler_params=PARAMS,
    )(face_port, tile_count, port_owner, *parts)


def pick_kernel(p2, m2, m3, p1, m1, here, out):
    near = [p1[0], here[0], m1[0], m2[0], m3[0]]
    far = [p2[0], p1[1], here[1], m1[1], m2[1]]
    for lean, tiles in enumerate((near, far)):
        tiles = [t.astype(f32) for t in tiles]
        full = [t < jnp.inf for t in tiles]
        run = full[0]
        for j in range(FACES):
            if j:
                run = run & full[j]
            x = jnp.where(run, tiles[j], tiles[j + 1])
            out[lean, j] = jnp.where(x < jnp.inf, x, 0.0).astype(bf16)


def pick(tiles):
    rows, rank = tiles[0].shape[1:]
    return pl.pallas_call(
        pick_kernel,
        out_shape=jax.ShapeDtypeStruct((2, FACES, rows, rank), bf16),
        in_specs=[VM] * 6,
        out_specs=VM,
        compiler_params=PARAMS,
    )(*tiles)


def panel(t0):
    lane = lax.broadcasted_iota(jnp.int32, (B, 128), 1)
    row = lax.broadcasted_iota(jnp.int32, (B, 128), 0)
    t1 = ((lane % B) == row).astype(f32)
    groups = B // 8
    r0 = [t0[8 * i : 8 * i + 8] for i in range(groups)]
    r1 = [t1[8 * i : 8 * i + 8] for i in range(groups)]
    half, row8 = jnp.where(lane < B, 0, B)[:8], row[:8]

    def column(block, c):
        return jnp.take_along_axis(block, half + c, axis=1, mode="promise_in_bounds")

    done = []
    ahead = [[column(r0[0], j)] for j in range(8)]
    for g in range(groups):
        n = groups - g
        cur = [
            [ahead[j][-1]] + [column(r0[g + i], 8 * g + j) for i in range(1, n)] for j in range(8)
        ]
        ahead = []
        if n > 1:
            ahead = [[column(r0[g + i], 8 * g + 8 + j) for i in range(2)] for j in range(8)]
        for j in range(0, 8, 2):
            cj, ck = cur[j], cur[j + 1]
            a, b, d = cj[0][j : j + 1], cj[0][j + 1 : j + 2], ck[0][j + 1 : j + 2]
            det = a * d - b * b
            inv = pl.reciprocal(det, approx=True)
            inv = inv * (2.0 - det * inv)
            m0 = [x * d - y * b for x, y in zip(cj, ck)]
            m1 = [y * a - x * b for x, y in zip(cj, ck)]
            m0[0] = jnp.where(row8 > j + 1, m0[0], 0.0)
            m1[0] = jnp.where(row8 > j + 1, m1[0], 0.0)

            def swept(top, blocks):
                p, q = top[j : j + 1] * inv, top[j + 1 : j + 2] * inv
                return [c - (x * p + y * q) for c, x, y in zip(blocks, m0, m1)]

            for k in range(j + 2, 8):
                cur[k] = swept(cur[k][0], cur[k])
            ahead = [swept(c[0], c) for c in ahead]
            done.append((a, b, d, r1[g][j : j + 1], r1[g][j + 1 : j + 2]))
            r0[g:] = swept(r0[g], r0[g:])
            r1[g:] = swept(r1[g], r1[g:])
    rows = []
    for a, b, d, p1, q1 in done:
        l10 = b * (1.0 / a)
        rows.append(p1 * lax.rsqrt(a))
        rows.append((q1 - l10 * p1) * lax.rsqrt(d - b * l10))
    return jnp.concatenate(rows, axis=0)


def solve_kernel(owner, x0, x1, x2, x3, o_hbm, x_ref, o_ref, sem):
    me = lax.axis_index("mesh")
    s = lax.axis_index("samp")
    ports = owner.shape[0]
    near, far = lax.rem(me - 1 + ports, ports), lax.rem(me - 2 + ports, ports)
    both = (owner[near] == me) & (owner[far] == me)
    near_first = jnp.where(both, near < far, owner[near] == me)
    slots = (jnp.where(near_first, 0, 1), jnp.where(near_first, 1, 0))
    n = x0.shape[3]
    rows = x0.shape[2]
    each = FACES * rows
    row = lax.broadcasted_iota(jnp.int32, (n, n), 0)
    col = lax.broadcasted_iota(jnp.int32, (n, n), 1)
    eye = (row == col).astype(f32)
    blocks = []
    for p in range(2):
        for k, x in enumerate((x0, x1, x2, x3)):
            x_ref[p, k * each : (k + 1) * each] = x[p].reshape(each, n)
        x = x_ref[p]
        g = mm(x, x, ((0,), (0,)), None)
        g = g + (0.1 * jnp.sum(g * eye) / n + 1e-6) * eye
        blocks.append([g[k * B : (k + 1) * B] for k in range(n // B)])
    col, row = col[:B], row[:B]
    stores = []

    def finish(k):
        wide = 2 * B
        here = pl.ds((k - 1) * B, wide)
        depth = (k + 1) * B
        for p in range(2):
            w = [jnp.where(col <= row + i * B, blocks[p][i], 0.0) for i in (k - 1, k)]
            w = jnp.concatenate(w, axis=0)[:, :depth]
            w0 = w.astype(bf16)
            e = w - w0.astype(f32)
            w1 = e.astype(bf16)
            w2 = (e - w1.astype(f32)).astype(bf16)
            x = x_ref[p, :, :depth]
            y = mm(x, w2, ((1,), (1,)), None) + mm(x, w1, ((1,), (1,)), None)
            y = y + mm(x, w0, ((1,), (1,)), None)
            for t in range(QUARTERS):
                q = lax.rem(s - TURNS[t] + QUARTERS, QUARTERS)
                for j in range(FACES):
                    at = pl.multiple_of(j * QUARTERS * rows + q * rows, rows)
                    o_ref[p, pl.ds(at, rows), here] = y[t * each + j * rows : t * each + (j + 1) * rows]
            store = pltpu.make_async_copy(
                o_ref.at[p, :, here], o_hbm.at[slots[p], :, here], sem.at[p, k // 2]
            )
            store.start()
            stores.append(store)

    for k in range(n // B):
        lo, hi = k * B, (k + 1) * B
        inside = (col >= lo) & (col < hi)
        t = panel(jnp.concatenate([x[k][:, lo:hi] for x in blocks], axis=1))
        ys = []
        for p in range(2):
            w = t[:, p * B : (p + 1) * B]
            sk = jnp.where(inside, (col - lo == row).astype(f32), blocks[p][k])
            blocks[p][k] = mm(w, sk)
            ys.append(w)
        for i in range(k + 1, n // B):
            for p in range(2):
                u = mm(blocks[p][i][:, lo:hi], ys[p], ((1,), (1,)))
                blocks[p][i] = jnp.where(inside, 0.0, blocks[p][i]) - mm(u, blocks[p][k])
        if k % 2:
            finish(k)
    for store in stores:
        store.wait()


def solve(port_owner, pieces):
    rows, n = pieces[0].shape[2:]
    height = FACES * QUARTERS * rows
    return pl.pallas_call(
        solve_kernel,
        out_shape=jax.ShapeDtypeStruct((2, height, n), f32),
        in_specs=[SM] + [VM] * QUARTERS,
        out_specs=ANY,
        scratch_shapes=[
            pltpu.VMEM((2, height, n), bf16),
            pltpu.VMEM((2, height, n), f32),
            pltpu.SemaphoreType.DMA((2, 2)),
        ],
        compiler_params=PARAMS,
    )(port_owner, *pieces)


def body(traces, sketch, face_port, face_pos, tile_count, port_owner):
    (k2,) = sketch_parts(traces, sketch, (2,))
    k1, k3, own = sketch_parts(traces, sketch, (1, 3, 0))
    k2 = shifted(k2, "samp", 2)
    k1 = shifted(k1, "samp", 1)
    k3 = shifted(k3, "samp", -1)
    *sends, here = place(face_port, tile_count, port_owner, (own, k1, k2, k3))
    tiles = [shifted(x, "mesh", distance) for x, distance in zip(sends, ROUTES)]
    mine = pick((*tiles, here))
    pieces = [mine] + [shifted(mine, "samp", k) for k in TURNS[1:]]
    return solve(port_owner, pieces)


def solution(mesh):
    placed = (P("mesh", None, "samp"), P("samp", None), P("mesh"), P("mesh"), P("mesh"), P())
    return jax.shard_map(
        body, mesh=mesh, in_specs=placed, out_specs=P("mesh", None, None), check_vma=False
    )
```

```python
import functools

import jax
import jax.numpy as jnp
from jax import lax
from jax.experimental import pallas as pl
from jax.experimental.pallas import tpu as pltpu
from jax.sharding import PartitionSpec as P

FACES = 4
QUARTERS = 4
SPAN = 5
B = 64
HI = lax.Precision.HIGHEST
f32 = jnp.float32
bf16 = jnp.bfloat16
VM = pl.BlockSpec(memory_space=pltpu.VMEM)
SM = pl.BlockSpec(memory_space=pltpu.SMEM)
ANY = pl.BlockSpec(memory_space=pltpu.HBM)
PARAMS = pltpu.CompilerParams(vmem_limit_bytes=24 << 20)
WIDE = pltpu.CompilerParams(vmem_limit_bytes=54300 << 10)
TURNS = (0, 3, 1, 2)
ROUTES = (2, -2, -3, 1, -1)


def shifted(block, axis, distance):
    n = lax.axis_size(axis)
    return lax.ppermute(block, axis, [(i, (i + distance) % n) for i in range(n)])


def mm(a, b, dims=((1,), (0,)), prec=HI):
    return lax.dot_general(a, b, (dims, ((), ())), precision=prec, preferred_element_type=f32)


def sketch_kernel(turns, t_hbm, r_hbm, *refs):
    outs, (t, r, sem) = refs[: len(turns)], refs[len(turns) :]
    s = lax.axis_index("samp")
    slots, rows = outs[0].shape[:2]
    load_r = pltpu.make_async_copy(r_hbm, r, sem.at[len(turns)])
    load_r.start()
    loads = []
    for i, k in enumerate(turns):
        c = lax.rem(s + k, QUARTERS)
        load = pltpu.make_async_copy(
            t_hbm.at[:, pl.ds(pl.multiple_of(c * rows, rows), rows), :], t.at[i], sem.at[i]
        )
        load.start()
        loads.append(load)
    load_r.wait()
    for i, load in enumerate(loads):
        load.wait()
        y = mm(t[i].reshape(slots * rows, t.shape[3]), r[...], prec=None)
        outs[i][...] = y.reshape(outs[i].shape)


def sketch_parts(traces, sketch, turns):
    slots, cells, samples = traces.shape
    rows = cells // QUARTERS
    rank = sketch.shape[1]
    part = jax.ShapeDtypeStruct((slots, rows, rank), f32)
    return pl.pallas_call(
        functools.partial(sketch_kernel, turns),
        out_shape=[part] * len(turns),
        in_specs=[ANY, ANY],
        out_specs=[VM] * len(turns),
        scratch_shapes=[
            pltpu.VMEM((len(turns), slots, rows, samples), bf16),
            pltpu.VMEM((samples, rank), bf16),
            pltpu.SemaphoreType.DMA((len(turns) + 1,)),
        ],
        compiler_params=WIDE,
    )(traces, sketch)


def place_kernel(port, count, owner, a, b, c, d, p2, m2, m3, p1, m1, here, total):
    me = lax.axis_index("mesh")
    n = owner.shape[0]
    total[...] = ((a[...] + b[...]) + (c[...] + d[...])).astype(bf16)
    sends = {}
    for dist in range(SPAN):
        p = lax.rem(me - dist + n, n)
        lean = lax.rem(owner[p] - p + n, n)
        slot = jnp.int32(-1)
        for i in range(total.shape[0]):
            slot = jnp.where((port[i] == p) & (i < count[0]), i, slot)
        sends[dist] = (slot, lean)

    def tile(dist, lean):
        slot, its = sends[dist]
        good = (slot >= 0) & (its == lean)
        return jnp.where(good, total[jnp.maximum(slot, 0)], jnp.inf).astype(bf16)

    for out, near in ((p1, 0), (here, 1), (m1, 2), (m2, 3)):
        out[0] = tile(near, 1)
        out[1] = tile(near + 1, 2)
    p2[0] = tile(0, 2)
    m3[0] = tile(4, 1)
    p2[1] = p2[0]
    m3[1] = m3[0]


def place(face_port, tile_count, port_owner, parts):
    slots, rows, rank = parts[0].shape
    two = jax.ShapeDtypeStruct((2, rows, rank), bf16)
    return pl.pallas_call(
        place_kernel,
        out_shape=[two] * 6,
        in_specs=[SM] * 3 + [VM] * 4,
        out_specs=[VM] * 6,
        scratch_shapes=[pltpu.VMEM((slots, rows, rank), bf16)],
        compiler_params=PARAMS,
    )(face_port, tile_count, port_owner, *parts)


def pick_kernel(p2, m2, m3, p1, m1, here, out):
    near = [p1[0], here[0], m1[0], m2[0], m3[0]]
    far = [p2[0], p1[1], here[1], m1[1], m2[1]]
    for lean, tiles in enumerate((near, far)):
        tiles = [t.astype(f32) for t in tiles]
        full = [t < jnp.inf for t in tiles]
        run = full[0]
        for j in range(FACES):
            if j:
                run = run & full[j]
            x = jnp.where(run, tiles[j], tiles[j + 1])
            out[lean, j] = jnp.where(x < jnp.inf, x, 0.0).astype(bf16)


def pick(tiles):
    rows, rank = tiles[0].shape[1:]
    return pl.pallas_call(
        pick_kernel,
        out_shape=jax.ShapeDtypeStruct((2, FACES, rows, rank), bf16),
        in_specs=[VM] * 6,
        out_specs=VM,
        compiler_params=PARAMS,
    )(*tiles)


def panel(t0):
    lane = lax.broadcasted_iota(jnp.int32, (B, 128), 1)
    row = lax.broadcasted_iota(jnp.int32, (B, 128), 0)
    t1 = ((lane % B) == row).astype(f32)
    groups = B // 8
    r0 = [t0[8 * i : 8 * i + 8] for i in range(groups)]
    r1 = [t1[8 * i : 8 * i + 8] for i in range(groups)]
    half, row8 = jnp.where(lane < B, 0, B)[:8], row[:8]

    def column(block, c):
        return jnp.take_along_axis(block, half + c, axis=1, mode="promise_in_bounds")

    done = []
    ahead = [[column(r0[0], j)] for j in range(8)]
    for g in range(groups):
        n = groups - g
        cur = [
            [ahead[j][-1]] + [column(r0[g + i], 8 * g + j) for i in range(1, n)] for j in range(8)
        ]
        ahead = []
        if n > 1:
            ahead = [[column(r0[g + i], 8 * g + 8 + j) for i in range(2)] for j in range(8)]
        for j in range(0, 8, 2):
            cj, ck = cur[j], cur[j + 1]
            a, b, d = cj[0][j : j + 1], cj[0][j + 1 : j + 2], ck[0][j + 1 : j + 2]
            det = a * d - b * b
            inv = pl.reciprocal(det, approx=True)
            inv = inv * (2.0 - det * inv)
            m0 = [x * d - y * b for x, y in zip(cj, ck)]
            m1 = [y * a - x * b for x, y in zip(cj, ck)]
            m0[0] = jnp.where(row8 > j + 1, m0[0], 0.0)
            m1[0] = jnp.where(row8 > j + 1, m1[0], 0.0)

            def swept(top, blocks):
                p, q = top[j : j + 1] * inv, top[j + 1 : j + 2] * inv
                return [c - (x * p + y * q) for c, x, y in zip(blocks, m0, m1)]

            for k in range(j + 2, 8):
                cur[k] = swept(cur[k][0], cur[k])
            ahead = [swept(c[0], c) for c in ahead]
            done.append((a, b, d, r1[g][j : j + 1], r1[g][j + 1 : j + 2]))
            r0[g:] = swept(r0[g], r0[g:])
            r1[g:] = swept(r1[g], r1[g:])
    rows = []
    for a, b, d, p1, q1 in done:
        l10 = b * (1.0 / a)
        rows.append(p1 * lax.rsqrt(a))
        rows.append((q1 - l10 * p1) * lax.rsqrt(d - b * l10))
    return jnp.concatenate(rows, axis=0)


def solve_kernel(owner_hbm, x0, x1, x2, x3, o_hbm, x_ref, o_ref, owner, sem, owner_sem):
    table = pltpu.make_async_copy(owner_hbm, owner, owner_sem)
    table.start()
    me = lax.axis_index("mesh")
    s = lax.axis_index("samp")
    slots = []
    n = x0.shape[3]
    rows = x0.shape[2]
    each = FACES * rows
    row = lax.broadcasted_iota(jnp.int32, (n, n), 0)
    col = lax.broadcasted_iota(jnp.int32, (n, n), 1)
    eye = (row == col).astype(f32)
    blocks = []
    for p in range(2):
        for k, x in enumerate((x0, x1, x2, x3)):
            x_ref[p, k * each : (k + 1) * each] = x[p].reshape(each, n)
        x = x_ref[p]
        g = mm(x, x, ((0,), (0,)), None)
        g = g + (0.1 * jnp.sum(g * eye) / n + 1e-6) * eye
        blocks.append([g[k * B : (k + 1) * B] for k in range(n // B)])
    col, row = col[:B], row[:B]
    stores = []

    def finish(k):
        wide = 2 * B
        here = pl.ds((k - 1) * B, wide)
        depth = (k + 1) * B
        for p in range(2):
            w = [jnp.where(col <= row + i * B, blocks[p][i], 0.0) for i in (k - 1, k)]
            w = jnp.concatenate(w, axis=0)[:, :depth]
            w0 = w.astype(bf16)
            e = w - w0.astype(f32)
            w1 = e.astype(bf16)
            w2 = (e - w1.astype(f32)).astype(bf16)
            x = x_ref[p, :, :depth]
            y = mm(x, w2, ((1,), (1,)), None) + mm(x, w1, ((1,), (1,)), None)
            y = y + mm(x, w0, ((1,), (1,)), None)
            for t in range(QUARTERS):
                q = lax.rem(s - TURNS[t] + QUARTERS, QUARTERS)
                for j in range(FACES):
                    at = pl.multiple_of(j * QUARTERS * rows + q * rows, rows)
                    o_ref[p, pl.ds(at, rows), here] = y[t * each + j * rows : t * each + (j + 1) * rows]
            store = pltpu.make_async_copy(
                o_ref.at[p, :, here], o_hbm.at[slots[p], :, here], sem.at[p, k // 2]
            )
            store.start()
            stores.append(store)

    for k in range(n // B):
        lo, hi = k * B, (k + 1) * B
        inside = (col >= lo) & (col < hi)
        t = panel(jnp.concatenate([x[k][:, lo:hi] for x in blocks], axis=1))
        ys = []
        for p in range(2):
            w = t[:, p * B : (p + 1) * B]
            sk = jnp.where(inside, (col - lo == row).astype(f32), blocks[p][k])
            blocks[p][k] = mm(w, sk)
            ys.append(w)
        for i in range(k + 1, n // B):
            for p in range(2):
                u = mm(blocks[p][i][:, lo:hi], ys[p], ((1,), (1,)))
                blocks[p][i] = jnp.where(inside, 0.0, blocks[p][i]) - mm(u, blocks[p][k])
        if k == 1:
            table.wait()
            ports = owner.shape[0]
            near, far = lax.rem(me - 1 + ports, ports), lax.rem(me - 2 + ports, ports)
            both = (owner[near] == me) & (owner[far] == me)
            near_first = jnp.where(both, near < far, owner[near] == me)
            slots += [jnp.where(near_first, 0, 1), jnp.where(near_first, 1, 0)]
        if k % 2:
            finish(k)
    for store in stores:
        store.wait()


def solve(port_owner, pieces):
    rows, n = pieces[0].shape[2:]
    height = FACES * QUARTERS * rows
    return pl.pallas_call(
        solve_kernel,
        out_shape=jax.ShapeDtypeStruct((2, height, n), f32),
        in_specs=[ANY] + [VM] * QUARTERS,
        out_specs=ANY,
        scratch_shapes=[
            pltpu.VMEM((2, height, n), bf16),
            pltpu.VMEM((2, height, n), f32),
            pltpu.SMEM((port_owner.shape[0],), jnp.int32),
            pltpu.SemaphoreType.DMA((2, 2)),
            pltpu.SemaphoreType.DMA,
        ],
        compiler_params=PARAMS,
    )(port_owner, *pieces)


def body(traces, sketch, face_port, face_pos, tile_count, port_owner):
    (k2,) = sketch_parts(traces, sketch, (2,))
    k1, k3, own = sketch_parts(traces, sketch, (1, 3, 0))
    k2 = shifted(k2, "samp", 2)
    k1 = shifted(k1, "samp", 1)
    k3 = shifted(k3, "samp", -1)
    *sends, here = place(face_port, tile_count, port_owner, (own, k1, k2, k3))
    tiles = [shifted(x, "mesh", distance) for x, distance in zip(sends, ROUTES)]
    mine = pick((*tiles, here))
    pieces = [mine] + [shifted(mine, "samp", k) for k in TURNS[1:]]
    return solve(port_owner, pieces)


def solution(mesh):
    placed = (P("mesh", None, "samp"), P("samp", None), P("mesh"), P("mesh"), P("mesh"), P())
    return jax.shard_map(
        body, mesh=mesh, in_specs=placed, out_specs=P("mesh", None, None), check_vma=False
    )
```
